32 devices in a mesh: groups: 2 (over y), dp: 8 (over z, x), pipe: 2 (over core).
Axes of the slice: x: 2, y: 2, z: 4, core: 2. Of those that a mesh axis runs over, the one named last changes fastest.
Arguments:
- inputs: bfloat16 [2, 32, 256, 512], P('pipe', ('groups', 'dp')), parts along dimension 1, may hold values from -24 to 24
- out_grad: bfloat16 [2, 32, 256, 512], P('pipe', ('groups', 'dp')), parts along dimension 1, may hold values from -6 to 6
- lengths: int32 [2, 32], P('pipe', ('groups', 'dp')), parts along dimension 1, may hold values from 64 to 256, as said below
- master: float32 [2, 4096, 512], P('pipe', ('groups', 'dp')), parts along dimension 1, may hold values from -16 to 16
- moment_first: float32 [2, 4096, 512], P('pipe', ('groups', 'dp')), parts along dimension 1, may hold values from -16 to 16
- moment_second: float32 [2, 4096, 512], P('pipe', ('groups', 'dp')), parts along dimension 1, may hold values from 0.0005 to 2000
Outputs:
- new_master: float32 [2, 4096, 512], P('pipe', ('groups', 'dp')), parts along dimension 1
- new_first: float32 [2, 4096, 512], P('pipe', ('groups', 'dp')), parts along dimension 1
- new_second: float32 [2, 4096, 512], P('pipe', ('groups', 'dp')), parts along dimension 1
The draws below stay inside these ranges and needn't reach their ends.
There are 2 independent parts, one for each index of `groups`. The reference program is written for one: setup_inputs(seed, part) draws one part's arguments, and reference() takes and returns one part's arrays. A program takes and returns all parts, laid end to end along the dimension named above; each array names one. Nothing has to cross between parts.
Inputs may be any that keep to these rules, and one draw needn't show every extreme that they name: `lengths`: every draw has a sequence of all 256 tokens.
All inputs are finite; a program needn't handle non-finite values.
Results may differ from the reference program's by a relative error of at most 0.0055.
Values may be sent and summed in bfloat16 or wider, within the bound.
No kernel may reach another device: no remote copies, remote signals or barrier semaphores. Data moves between devices by JAX's collectives and lax.ppermute only.
A program may use at most 128 MiB of HBM per device.

```python
import math
import jax
import jax.numpy as jnp
from jax import lax

D = 512
HEAD = 64
L = 256
STEP = 10
SEQS = 16


def spread_scales(key, rows, cols, rise, top):
    key_rows, key_cols = jax.random.split(key)
    row_scale = jnp.exp(jax.random.uniform(key_rows, (2, rows, 1), jnp.float32) * math.log(top))
    col_scale = jnp.exp(jax.random.uniform(key_cols, (2, 1, cols), jnp.float32) * math.log(top))
    place = jnp.arange(rows).astype(jnp.float32) / rows
    lift = jnp.exp((place - 1.0) * math.log(rise))[None, :, None]
    return row_scale * col_scale * lift / top


def draw_master(key, part):
    key = jax.random.fold_in(key, 11)
    key_base, key_scale = jax.random.split(key)
    base = jnp.clip(jax.random.normal(key_base, (2, 4 * D, D), jnp.float32), -4.0, 4.0)
    scales = spread_scales(key_scale, 4 * D, D, 8.0, 10.0)
    return jnp.clip(base * scales, -16.0, 16.0)


def draw_moment_first(key, part):
    key = jax.random.fold_in(key, 12)
    key_base, key_scale = jax.random.split(key)
    base = jnp.clip(jax.random.normal(key_base, (2, 4 * D, D), jnp.float32), -4.0, 4.0)
    scales = spread_scales(key_scale, 4 * D, D, 8.0, 10.0)
    return jnp.clip(base * scales, -16.0, 16.0)


def draw_moment_second(key, part):
    key = jax.random.fold_in(key, 13)
    key_base, key_scale = jax.random.split(key)
    base = jnp.exp(jax.random.uniform(key_base, (2, 4 * D, D), jnp.float32, math.log(0.25), math.log(4.0)))
    scales = spread_scales(key_scale, 4 * D, D, 8.0, 10.0)
    return jnp.clip(base * scales * scales, 0.0005, 2000.0)


def draw_inputs(key, part):
    key = jax.random.fold_in(key, 14)
    key_base = jax.random.fold_in(key, 0)
    values = jnp.clip(jax.random.normal(key_base, (2, SEQS, L, D), jnp.float32), -6.0, 6.0)
    return jnp.clip(values, -24.0, 24.0).astype(jnp.bfloat16)


def draw_lengths(key, part):
    key = jax.random.fold_in(key, 15)
    key_values, key_place = jax.random.split(key)
    values = jax.random.randint(key_values, (2 * SEQS,), L // 4, L + 1)
    place = jax.random.randint(key_place, (), 0, 2 * SEQS)
    values = jnp.where(jnp.arange(2 * SEQS) == place, L, values)
    return values.reshape(2, SEQS).astype(jnp.int32)


def block_scale(key, shape, cuts, least, largest):
    level, own = 1.0, jax.random.fold_in(key, 6)
    for dim, blocks in cuts:
        steps = jnp.exp(jax.random.uniform(jax.random.fold_in(own, dim), (blocks,), jnp.float32, least / len(cuts), largest / len(cuts)))
        level = level * jnp.repeat(steps, shape[dim] // blocks).reshape([-1 if axis == dim else 1 for axis in range(len(shape))])
    return level


def normal_values(stream_key, extent, scale, most, shards=(), dtype=jnp.bfloat16):
    array = scale * jax.random.normal(stream_key, extent, jnp.float32)
    if shards:
        array = array * block_scale(stream_key, extent, shards, -0.22, 0.18)
    return jnp.clip(array, -most, most).astype(dtype)


def setup_inputs(seed: int = 0, part: int = 0) -> dict:
    arg_keys = jax.random.split(jax.random.key(seed), 7)
    part_splits = jax.random.split(jax.random.fold_in(arg_keys[6], part), 7)
    return {
        "inputs": draw_inputs(jax.random.fold_in(jax.random.fold_in(arg_keys[6], part), 71), part),
        "out_grad": normal_values(part_splits[1], (2, SEQS, L, D), 1.0, 6.0, ((0, 2), (1, 8))),
        "lengths": draw_lengths(jax.random.fold_in(jax.random.fold_in(arg_keys[6], part), 71), part),
        "master": draw_master(jax.random.fold_in(jax.random.fold_in(arg_keys[6], part), 71), part),
        "moment_first": draw_moment_first(jax.random.fold_in(jax.random.fold_in(arg_keys[6], part), 71), part),
        "moment_second": draw_moment_second(jax.random.fold_in(jax.random.fold_in(arg_keys[6], part), 71), part),
    }


def layer_norm(resid):
    centre = resid - lax.optimization_barrier(jnp.mean(resid, axis=-1, keepdims=True))
    return centre * lax.rsqrt(lax.optimization_barrier(jnp.mean(centre * centre, axis=-1, keepdims=True)) + 1e-05)

def attention(query, keys, values, live):
    length, width = query.shape
    heads = width // HEAD
    q_full = query.astype(jnp.float32).reshape(length, heads, HEAD)
    k_full = keys.astype(jnp.float32).reshape(length, heads, HEAD)
    v_full = values.astype(jnp.float32).reshape(length, heads, HEAD)
    scores = jnp.einsum('qhd,khd->hqk', q_full, k_full) * HEAD ** (-0.5)
    keep = jnp.arange(length) < live
    scores = jnp.where(keep[None, None, :], scores, -1e+30)
    scores = scores - lax.optimization_barrier(jnp.max(scores, axis=-1, keepdims=True))
    expo = jnp.exp(scores)
    probs = expo / lax.optimization_barrier(jnp.sum(expo, axis=-1, keepdims=True))
    rounded = lax.optimization_barrier(probs.astype(jnp.bfloat16)).astype(jnp.float32)
    mixed = jnp.einsum('hqk,khd->qhd', rounded, v_full)
    return mixed.reshape(length, width).astype(jnp.bfloat16)

def section_forward(weights, inputs, live):
    width = inputs.shape[1]
    factor = width ** (-0.5)
    query = (jnp.dot(inputs, weights[:width], preferred_element_type=jnp.float32) * factor).astype(jnp.bfloat16)
    keys = (jnp.dot(inputs, weights[width:2 * width], preferred_element_type=jnp.float32) * factor).astype(jnp.bfloat16)
    values = (jnp.dot(inputs, weights[2 * width:3 * width], preferred_element_type=jnp.float32) * factor).astype(jnp.bfloat16)
    mixed = attention(query, keys, values, live)
    resid = inputs.astype(jnp.float32) + jnp.dot(mixed, weights[3 * width:], preferred_element_type=jnp.float32) * factor
    return (layer_norm(resid).astype(jnp.bfloat16), (inputs, query, keys, values, mixed, resid))

def section_backward(weights, saved, grad_out, live, want_input):
    inputs, query, keys, values, mixed, resid = saved
    width = inputs.shape[1]
    factor = width ** (-0.5)
    _, norm_back = jax.vjp(layer_norm, resid)
    grad_resid = norm_back(grad_out.astype(jnp.float32))[0]
    grad_attn = grad_resid.astype(jnp.bfloat16)
    grad_wo = jnp.dot(mixed.T, grad_attn, preferred_element_type=jnp.float32) * factor
    grad_mixed = (jnp.dot(grad_attn, weights[3 * width:].T, preferred_element_type=jnp.float32) * factor).astype(jnp.bfloat16)
    _, core_back = jax.vjp(lambda a, b, c: attention(a, b, c, live), query, keys, values)
    grad_q, grad_k, grad_v = core_back(grad_mixed)
    grad_wq = jnp.dot(inputs.T, grad_q, preferred_element_type=jnp.float32) * factor
    grad_wk = jnp.dot(inputs.T, grad_k, preferred_element_type=jnp.float32) * factor
    grad_wv = jnp.dot(inputs.T, grad_v, preferred_element_type=jnp.float32) * factor
    grads = jnp.concatenate([grad_wq, grad_wk, grad_wv, grad_wo], axis=0).astype(jnp.float32)
    if want_input:
        back = jnp.dot(grad_q, weights[:width].T, preferred_element_type=jnp.float32)
        back = back + jnp.dot(grad_k, weights[width:2 * width].T, preferred_element_type=jnp.float32)
        back = back + jnp.dot(grad_v, weights[2 * width:3 * width].T, preferred_element_type=jnp.float32)
        return ((grad_resid + back * factor).astype(jnp.bfloat16), grads)
    return (None, grads)

def lamb_update(weights, first, second, grads):
    new_first = 0.9 * first + 0.1 * grads
    new_second = 0.999 * second + 0.001 * grads * grads
    corrected = new_first / (1.0 - 0.9 ** STEP)
    spread = new_second / (1.0 - 0.999 ** STEP)
    update = corrected / (jnp.sqrt(spread) + 1e-06) + 0.05 * weights
    weight_sq = jnp.sum(weights * weights)
    update_sq = jnp.sum(update * update)
    trust = jnp.sqrt(weight_sq) / (jnp.sqrt(update_sq) + 1e-06)
    return (weights - 0.05 * trust * update, new_first, new_second)

def reference(inputs, out_grad, lengths, master, moment_first, moment_second):
    inputs = inputs.astype(jnp.bfloat16)
    out_grad = out_grad.astype(jnp.bfloat16)
    master = master.astype(jnp.float32)
    moment_first = moment_first.astype(jnp.float32)
    moment_second = moment_second.astype(jnp.float32)
    leading = master[0].astype(jnp.bfloat16)
    trailing = master[1].astype(jnp.bfloat16)
    flat_inputs = inputs.reshape(2 * SEQS, L, D)
    flat_targets = out_grad[::-1].reshape(2 * SEQS, L, D)
    flat_live = lengths.reshape(2 * SEQS).astype(jnp.int32)
    positions = jnp.arange(L).astype(jnp.int32)

    def one(carry, item):
        sequence, target, live = item
        hidden, saved_lead = section_forward(leading, sequence, live)
        _, saved_trail = section_forward(trailing, hidden, live)
        target = jnp.where((positions < live)[:, None], target, jnp.zeros_like(target))
        back, grad_trail = section_backward(trailing, saved_trail, target, live, True)
        _, grad_lead = section_backward(leading, saved_lead, back, live, False)
        return ((carry[0] + grad_lead, carry[1] + grad_trail), None)
    empty = jnp.zeros((4 * D, D), jnp.float32)
    (grad_lead, grad_trail), _ = lax.scan(one, (empty, empty), (flat_inputs, flat_targets, flat_live))
    master_a, first_a, second_a = lamb_update(master[0], moment_first[0], moment_second[0], grad_lead)
    master_b, first_b, second_b = lamb_update(master[1], moment_first[1], moment_second[1], grad_trail)
    return (jnp.stack([master_a, master_b]), jnp.stack([first_a, first_b]), jnp.stack([second_a, second_b]))
```

```python
import functools

import jax
import jax.numpy as jnp
from jax import lax
from jax.experimental import pallas as pl
from jax.experimental.pallas import tpu as pltpu
from jax.sharding import PartitionSpec as P

HEAD = 64
PAIR = 128
STEP = 10
F32 = jnp.float32
BF16 = jnp.bfloat16


def dot(a, b):
    return lax.dot_general(a, b, (((1,), (0,)), ((), ())), preferred_element_type=F32)


def dot_nt(a, b):
    return lax.dot_general(a, b, (((1,), (1,)), ((), ())), preferred_element_type=F32)


def half_masks(length):
    lane = lax.broadcasted_iota(jnp.int32, (length, PAIR), 1)
    return lane < HEAD, lane >= HEAD


def forward(sec, micro, length, width, scal, x_ref, w, q, k, v, v_t, p, mixed_t, xhat, rstd, h_ref):
    factor = width ** (-0.5)
    pairs = width // PAIR
    x2 = x_ref[...]
    q[sec] = (dot(x2, w[sec, 0:width]) * factor).astype(BF16) * jnp.asarray(HEAD ** (-0.5), BF16)
    k[sec] = (dot(x2, w[sec, width : 2 * width]) * factor).astype(BF16)
    values = (dot(x2, w[sec, 2 * width : 3 * width]) * factor).astype(BF16)
    v[sec] = values
    v_t[...] = values.T

    for seq in range(micro):
        live = scal[1 + seq]
        rows = slice(seq * length, (seq + 1) * length)

        def body(pair, carry):
            lanes = pl.ds(pl.multiple_of(pair * PAIR, PAIR), PAIR)
            kp = k[sec, rows, lanes]
            qp = q[sec, rows, lanes]
            masks = half_masks(length)
            keep = lax.broadcasted_iota(jnp.int32, (length, length), 0) < live
            parts = []
            for half in range(2):
                qm = jnp.where(masks[half], qp, jnp.zeros_like(qp))
                score = jnp.where(keep, dot_nt(kp, qm), -1e30)
                expo = jnp.exp(score - jnp.max(score, axis=0, keepdims=True))
                prob = expo * (1.0 / jnp.sum(expo, axis=0, keepdims=True))
                p[sec, seq * 2 * pairs + pair * 2 + half] = prob
                vh = v_t[pl.ds(pl.multiple_of(pair * PAIR + half * HEAD, HEAD), HEAD), rows]
                parts.append(dot(vh, prob.astype(BF16)))
            mixed_t[sec, lanes, rows] = jnp.concatenate(parts, axis=0).astype(BF16)
            return carry

        lax.fori_loop(0, pairs, body, 0)
    mixed = mixed_t[sec].T
    resid = x2.astype(F32) + dot(mixed, w[sec, 3 * width : 4 * width]) * factor
    centre = resid - jnp.mean(resid, axis=-1, keepdims=True)
    scale = lax.rsqrt(jnp.mean(centre * centre, axis=-1, keepdims=True) + 1e-05)
    normed = centre * scale
    xhat[sec] = normed
    rstd[sec] = jnp.broadcast_to(scale, rstd.shape[1:])
    if h_ref is not None:
        h_ref[...] = normed.astype(BF16)


def backward(sec, micro, length, width, grad, x_ref, w, q, k, v, k_t, p, mixed_t, xhat, rstd, dm, dq_t, dk, dv, emit, want):
    factor = width ** (-0.5)
    pairs = width // PAIR
    normed = xhat[sec]
    dres = rstd[sec][:, :1] * (
        grad
        - jnp.mean(grad, axis=-1, keepdims=True)
        - normed * jnp.mean(grad * normed, axis=-1, keepdims=True)
    )
    da = dres.astype(BF16)
    emit(sec, 3, dot(mixed_t[sec], da) * factor)
    dm[...] = (dot_nt(da, w[sec, 3 * width : 4 * width]) * factor).astype(BF16)
    k_t[...] = k[sec].T
    for seq in range(micro):
        rows = slice(seq * length, (seq + 1) * length)

        def body(pair, carry):
            lanes = pl.ds(pl.multiple_of(pair * PAIR, PAIR), PAIR)
            vp = v[sec, rows, lanes]
            qp = q[sec, rows, lanes]
            gp = dm[rows, lanes]
            masks = half_masks(length)
            parts = []
            gv = jnp.zeros((length, PAIR), F32)
            gk = jnp.zeros((length, PAIR), F32)
            for half in range(2):
                gm = jnp.where(masks[half], gp, jnp.zeros_like(gp))
                qm = jnp.where(masks[half], qp, jnp.zeros_like(qp))
                dp = dot_nt(vp, gm).astype(BF16).astype(F32)
                prob = p[sec, seq * 2 * pairs + pair * 2 + half]
                gv += dot(prob.astype(BF16), gm)
                total = jnp.sum(prob * dp, axis=0, keepdims=True)
                ds = (prob * (dp - total)).astype(BF16)
                gk += dot(ds, qm)
                kh = k_t[pl.ds(pl.multiple_of(pair * PAIR + half * HEAD, HEAD), HEAD), rows]
                parts.append(dot(kh, ds))
            dv[rows, lanes] = gv.astype(BF16)
            dk[rows, lanes] = gk.astype(BF16)
            dq_t[lanes, rows] = (jnp.concatenate(parts, axis=0) * HEAD ** (-0.5)).astype(BF16)
            return carry

        lax.fori_loop(0, pairs, body, 0)
    dq = dq_t[...].T
    x_t = x_ref[...].T
    emit(sec, 0, dot(x_t, dq) * factor)
    emit(sec, 1, dot(x_t, dk[...]) * factor)
    emit(sec, 2, dot(x_t, dv[...]) * factor)
    if not want:
        return None
    back = dot_nt(dq, w[sec, 0:width])
    back += dot_nt(dk[...], w[sec, width : 2 * width])
    back += dot_nt(dv[...], w[sec, 2 * width : 3 * width])
    return (dres + back * factor).astype(BF16)


def layers(micro, length, width, rows, places, scal, x_ref, g_ref, *refs):
    count = len(places)
    own_w, other_w = refs[:count], refs[count : 2 * count]
    own_g, other_g = refs[2 * count : 2 * count + 2]
    w, hid, q, k, v, tr, p, mixed_t, xhat, rstd, dm, dq_t, dk, dv = refs[2 * count + 2 :]
    side = scal[0]
    base = 1 + micro

    for group, sec in ((own_w, side), (other_w, 1 - side)):
        for (slot, shift), ref in zip(places, group):
            if rows:
                at = pl.multiple_of(scal[base + slot] * rows + shift, 16)
            else:
                at = 0
            w[sec, pl.ds(at, ref.shape[0])] = ref[...]

    def emit(sec, part, value):
        for b in range(width // rows if rows else 1):
            size = rows if rows else width
            if rows:
                index = part * (width // rows) + b
                at = pl.multiple_of(scal[base + 4 * width // rows + index] * rows, 16)
            else:
                at = part * width
            block = value[b * size : (b + 1) * size]

            @pl.when(side == sec)
            def _():
                own_g[pl.ds(at, size)] = block

            @pl.when(side != sec)
            def _():
                other_g[pl.ds(at, size)] = block.astype(BF16)

    dims = (micro, length, width)
    forward(0, *dims, scal, x_ref, w, q, k, v, tr, p, mixed_t, xhat, rstd, hid)
    forward(1, *dims, scal, hid, w, q, k, v, tr, p, mixed_t, xhat, rstd, None)
    pieces = []
    for seq in range(micro):
        pos = lax.broadcasted_iota(jnp.int32, (length, width), 0)
        piece = g_ref[seq * length : (seq + 1) * length].astype(F32)
        pieces.append(jnp.where(pos < scal[1 + seq], piece, 0.0))
    grad = jnp.concatenate(pieces, axis=0)
    back = backward(1, *dims, grad, hid, w, q, k, v, tr, p, mixed_t, xhat, rstd, dm, dq_t, dk, dv, emit, True)
    backward(0, *dims, back.astype(F32), x_ref, w, q, k, v, tr, p, mixed_t, xhat, rstd, dm, dq_t, dk, dv, emit, False)


def run_layers(scal, x, target, own, other, places, rows, micro, length, width):
    tokens = micro * length
    heads = width // HEAD
    vmem = pl.BlockSpec(memory_space=pltpu.VMEM)
    return pl.pallas_call(
        functools.partial(layers, micro, length, width, rows, places),
        out_shape=(
            jax.ShapeDtypeStruct((4 * width, width), F32),
            jax.ShapeDtypeStruct((4 * width, width), BF16),
        ),
        in_specs=[pl.BlockSpec(memory_space=pltpu.SMEM)] + [vmem] * (2 + 2 * len(own)),
        out_specs=(vmem, vmem),
        scratch_shapes=[
            pltpu.VMEM((2, 4 * width, width), BF16),
            pltpu.VMEM((tokens, width), BF16),
            pltpu.VMEM((2, tokens, width), BF16),
            pltpu.VMEM((2, tokens, width), BF16),
            pltpu.VMEM((2, tokens, width), BF16),
            pltpu.VMEM((width, tokens), BF16),
            pltpu.VMEM((2, micro * heads, length, length), F32),
            pltpu.VMEM((2, width, tokens), BF16),
            pltpu.VMEM((2, tokens, width), F32),
            pltpu.VMEM((2, tokens, PAIR), F32),
            pltpu.VMEM((tokens, width), BF16),
            pltpu.VMEM((width, tokens), BF16),
            pltpu.VMEM((tokens, width), BF16),
            pltpu.VMEM((tokens, width), BF16),
        ],
        compiler_params=pltpu.CompilerParams(vmem_limit_bytes=52 * 1024 * 1024),
    )(scal, x, target, *own, *other)


def swapped(value):
    return lax.ppermute(value, "pipe", [(0, 1), (1, 0)])


def ring_order(count):
    return list(range(0, count, 2)) + list(range(count - 1, 0, -2))


def on_device(inputs, out_grad, lengths, master, moment_first, moment_second):
    side = lax.axis_index("pipe")
    place = lax.axis_index("dp")
    count = lax.axis_size("dp")
    weights = master[0]
    rows, width = weights.shape
    micro, length = inputs.shape[1:3]
    ringed = count == 8 and rows % 32 == 0 and width % rows == 0
    ring = ring_order(count)
    onward = [(ring[i], ring[(i + 1) % count]) for i in range(count)]
    backward_way = [(b, a) for a, b in onward]

    def ahead(value):
        return lax.ppermute(value, "dp", onward)

    def behind(value):
        return lax.ppermute(value, "dp", backward_way)

    mine = weights.astype(BF16)
    target = swapped(out_grad[0]).reshape(micro * length, width)
    x = inputs[0].reshape(micro * length, width)
    scalars = [side[None], lengths[0]]
    half = rows // 2
    if ringed:
        own = [mine]
        places = [(0, 0)]
        fore, aft = mine, mine
        for step in range(1, count // 2):
            fore, aft = ahead(fore), behind(aft)
            own += [fore, aft]
            places += [(count - step, 0), (step, 0)]
        own += [ahead(fore[:half]), behind(aft[half:])]
        places += [(count // 2, 0), (count // 2, half)]
        position = jnp.asarray([ring.index(i) for i in range(count)], jnp.int32)
        me = position[place]
        scalars.append(jnp.asarray(ring, jnp.int32)[(me + jnp.arange(count, dtype=jnp.int32)) % count])
        scalars.append((position - me + count) % count)
    else:
        own = [lax.all_gather(mine, "dp", axis=0, tiled=True)]
        places = [(0, 0)]
    other = [swapped(value) for value in own]
    scal = jnp.concatenate([s.astype(jnp.int32) for s in scalars])
    own_g, other_g = run_layers(
        scal, x, target, own, other, places, rows if ringed else 0, micro, length, width
    )
    total = own_g + swapped(other_g).astype(F32)
    if ringed:
        mid = count // 2

        def block(index):
            return total[index * rows : (index + 1) * rows]

        fore = ahead(block(mid)[:half].astype(BF16)).astype(F32)
        aft = behind(block(mid)[half:].astype(BF16)).astype(F32)
        up, down = block(mid - 1), block(mid + 1)
        fore = jnp.concatenate([up[:half] + fore, up[half:]], axis=0)
        aft = jnp.concatenate([down[:half], down[half:] + aft], axis=0)
        for step in range(mid - 1, 0, -1):
            fore = ahead(fore.astype(BF16)).astype(F32)
            aft = behind(aft.astype(BF16)).astype(F32)
            if step > 1:
                fore = fore + block(step - 1)
                aft = aft + block(count - step + 1)
        grad_rows = block(0) + fore + aft
    else:
        grad_rows = lax.psum_scatter(total, "dp", scatter_dimension=0, tiled=True)
    new_first = 0.9 * moment_first[0] + 0.1 * grad_rows
    new_second = 0.999 * moment_second[0] + 0.001 * grad_rows * grad_rows
    corrected = new_first / (1.0 - 0.9**STEP)
    spread = new_second / (1.0 - 0.999**STEP)
    update = corrected / (jnp.sqrt(spread) + 1e-06) + 0.05 * weights
    squares = jnp.stack([jnp.sum(weights * weights), jnp.sum(update * update)])
    if ringed:
        hop = 1
        while hop < count:
            squares = squares + lax.ppermute(squares, "dp", [(i, i ^ hop) for i in range(count)])
            hop *= 2
    else:
        squares = lax.psum(squares, "dp")
    trust = jnp.sqrt(squares[0]) / (jnp.sqrt(squares[1]) + 1e-06)
    new_master = weights - 0.05 * trust * update
    return (new_master[None], new_first[None], new_second[None])


def solution(mesh):
    rows = P("pipe", ("groups", "dp"), None)
    in_specs = (
        P("pipe", ("groups", "dp"), None, None),
        P("pipe", ("groups", "dp"), None, None),
        P("pipe", ("groups", "dp")),
        rows,
        rows,
        rows,
    )
    return jax.shard_map(
        on_device, mesh=mesh, in_specs=in_specs, out_specs=(rows, rows, rows), check_vma=False
    )
```

```python
import functools

import jax
import jax.numpy as jnp
from jax import lax
from jax.experimental import pallas as pl
from jax.experimental.pallas import tpu as pltpu
from jax.sharding import PartitionSpec as P

HEAD = 64
PAIR = 128
AHEAD = 2
CUTS = 4
STEP = 10
F32 = jnp.float32
BF16 = jnp.bfloat16


def dot(a, b):
    return lax.dot_general(a, b, (((1,), (0,)), ((), ())), preferred_element_type=F32)


def dot_nt(a, b):
    return lax.dot_general(a, b, (((1,), (1,)), ((), ())), preferred_element_type=F32)


def padded(part, half):
    zero = jnp.zeros_like(part)
    return jnp.concatenate([part, zero] if half == 0 else [zero, part], axis=0)


def forward(sec, micro, length, width, live_ref, x_ref, w, q_t, k, v, tr, p, mixed_t, xhat, rstd, h_ref):
    factor = width ** (-0.5)
    x2 = x_ref[...]
    queries = (dot(x2, w[sec, 0:width]) * factor).astype(BF16) * jnp.asarray(HEAD ** (-0.5), BF16)
    q_t[sec] = queries.T
    k[sec] = (dot(x2, w[sec, width : 2 * width]) * factor).astype(BF16)
    values = (dot(x2, w[sec, 2 * width : 3 * width]) * factor).astype(BF16)
    v[sec] = values
    tr[...] = values.T
    lane = lax.broadcasted_iota(jnp.int32, (length, PAIR), 1)
    spot = lax.broadcasted_iota(jnp.int32, (length, PAIR), 0)
    first = (lax.broadcasted_iota(jnp.int32, (HEAD, length), 0) == 0).astype(F32).astype(BF16)
    heads = width // HEAD
    bias = [jnp.where(spot < live_ref[0, seq], 0.0, -1e30).astype(BF16) for seq in range(micro)]

    def scores(index):
        seq, head = divmod(index, heads)
        rows = slice(seq * length, (seq + 1) * length)
        kp = k[sec, rows, (head // 2) * PAIR : (head // 2 + 1) * PAIR]
        k_ext = jnp.where(lane == (0 if head % 2 else HEAD), bias[seq], kp)
        qh = q_t[sec, head * HEAD : (head + 1) * HEAD, rows]
        return dot(k_ext, jnp.concatenate([first, qh] if head % 2 else [qh, first], axis=0))

    waiting = [scores(index) for index in range(AHEAD)]
    for index in range(micro * heads):
        if index + AHEAD < micro * heads:
            waiting.append(scores(index + AHEAD))
        score = waiting.pop(0)
        seq, head = divmod(index, heads)
        rows = slice(seq * length, (seq + 1) * length)
        feats = slice(head * HEAD, (head + 1) * HEAD)
        expo = jnp.exp(score - jnp.max(score, axis=0, keepdims=True))
        prob = expo * (1.0 / jnp.sum(expo, axis=0, keepdims=True))
        p[sec, index] = prob
        mixed_t[sec, feats, rows] = dot(tr[feats, rows], prob.astype(BF16))
    mixed = mixed_t[sec].astype(BF16).T
    resid = x2.astype(F32) + dot(mixed, w[sec, 3 * width : 4 * width]) * factor
    centre = resid - jnp.mean(resid, axis=-1, keepdims=True)
    scale = lax.rsqrt(jnp.mean(centre * centre, axis=-1, keepdims=True) + 1e-05)
    normed = centre * scale
    xhat[sec] = normed
    rstd[sec] = jnp.broadcast_to(scale, rstd.shape[1:])
    if h_ref is not None:
        h_ref[...] = normed.astype(BF16)


def backward(sec, micro, length, width, grad, x_ref, w, q_t, k, v, tr, p, mixed_t, xhat, rstd, g_t, dq_t, dk, dv, emit, send):
    factor = width ** (-0.5)
    normed = xhat[sec]
    dres = rstd[sec][:, :1] * (
        grad
        - jnp.mean(grad, axis=-1, keepdims=True)
        - normed * jnp.mean(grad * normed, axis=-1, keepdims=True)
    )
    da = dres.astype(BF16)
    emit(sec, 3, dot(mixed_t[sec].astype(BF16), da) * factor)
    g_t[...] = (dot_nt(w[sec, 3 * width : 4 * width], da) * factor).astype(BF16)
    tr[...] = k[sec].T
    heads = width // HEAD

    def spread(index):
        seq, head = divmod(index, heads)
        rows = slice(seq * length, (seq + 1) * length)
        g_ext = padded(g_t[head * HEAD : (head + 1) * HEAD, rows], head % 2)
        return g_ext, dot(v[sec, rows, (head // 2) * PAIR : (head // 2 + 1) * PAIR], g_ext)

    waiting = [spread(index) for index in range(AHEAD)]
    for index in range(micro * heads):
        if index + AHEAD < micro * heads:
            waiting.append(spread(index + AHEAD))
        g_ext, dp = waiting.pop(0)
        seq, head = divmod(index, heads)
        rows = slice(seq * length, (seq + 1) * length)
        feats = slice(head * HEAD, (head + 1) * HEAD)
        q_ext = padded(q_t[sec, feats, rows], head % 2)
        delta = jnp.sum(mixed_t[sec, feats, rows] * g_t[feats, rows].astype(F32), axis=0, keepdims=True)
        prob = p[sec, index]
        ds = (prob * (dp - delta)).astype(BF16)
        gv_part = dot_nt(prob.astype(BF16), g_ext)
        gk_part = dot_nt(ds, q_ext)
        dq_t[feats, rows] = (dot(tr[feats, rows], ds) * HEAD ** (-0.5)).astype(BF16)
        if head % 2 == 0:
            gv, gk = gv_part, gk_part
        else:
            lanes = slice((head // 2) * PAIR, (head // 2 + 1) * PAIR)
            dv[rows, lanes] = (gv + gv_part).astype(BF16)
            dk[rows, lanes] = (gk + gk_part).astype(BF16)
    if send is not None:
        send(sec, (3,))
    dq = dq_t[...].T
    x_t = x_ref[...].T
    emit(sec, 0, dot(x_t, dq) * factor)
    emit(sec, 1, dot(x_t, dk[...]) * factor)
    if send is not None:
        send(sec, (0, 1))
    emit(sec, 2, dot(x_t, dv[...]) * factor)
    if send is not None:
        return None
    back = dot_nt(dq, w[sec, 0:width])
    back += dot_nt(dk[...], w[sec, width : 2 * width])
    back += dot_nt(dv[...], w[sec, 2 * width : 3 * width])
    return (dres + back * factor).astype(BF16)


def ring_spot(index, count):
    return jnp.where(index % 2 == 0, index // 2, count - 1 - index // 2)


def ring_index(spot, count):
    return jnp.where(spot < count // 2, 2 * spot, 2 * (count - 1 - spot) + 1)


def layers(micro, length, width, rows, count, places, live_in, x_in, g_in, *refs):
    size = len(places)
    own_w, other_w = refs[:size], refs[size : 2 * size]
    own_out, near_out, rest_out = refs[2 * size : 2 * size + 3]
    (live_ref, x_ref, g_ref, w, own_g, other_g, hid, q_t, k, v, tr, p, mixed_t, xhat, rstd, g_t, dq_t, dk, dv, in_sem, out_sem, act_sem) = refs[2 * size + 3 :]
    side = lax.axis_index("pipe")
    me = ring_spot(lax.axis_index("dp"), count)
    block = rows if rows else 4 * width
    live_copy = pltpu.make_async_copy(live_in, live_ref, act_sem.at[2])
    x_copy = pltpu.make_async_copy(x_in, x_ref, act_sem.at[0])
    g_copy = pltpu.make_async_copy(g_in, g_ref, act_sem.at[1])
    live_copy.start()
    x_copy.start()
    for sec, group in ((side, own_w), (1 - side, other_w)):
        for i, ((slot, shift), ref) in enumerate(zip(places, group)):
            at = pl.multiple_of(ring_index((me + slot) % count, count) * rows + shift, 16) if rows else 0
            pltpu.make_async_copy(ref, w.at[sec, pl.ds(at, ref.shape[0])], in_sem.at[sec, i]).start()
    tall = rows if rows else width
    g_copy.start()

    def turn_of(index):
        if not rows:
            return index
        return (ring_spot(jnp.int32(index), count) - me + count + count // 2) % count

    def emit(sec, part, value):
        for b in range(width // tall):
            here = pl.ds(pl.multiple_of(turn_of(part * (width // tall) + b) * tall, 16), tall)
            piece = value[b * tall : (b + 1) * tall]
            own_g[sec, here] = piece
            other_g[sec, here] = piece.astype(BF16)

    def send(sec, parts):
        for index in [part * (width // tall) + b for part in parts for b in range(width // tall)]:
            turn = turn_of(index)
            here = pl.ds(pl.multiple_of(turn * tall, 16), tall)

            @pl.when(side == sec)
            def _():
                pltpu.make_async_copy(own_g.at[sec, here], own_out.at[here], out_sem.at[0, index]).start()

            @pl.when((side != sec) & (turn == 0))
            def _():
                pltpu.make_async_copy(other_g.at[sec, here], near_out, out_sem.at[1, index]).start()

            @pl.when((side != sec) & (turn != 0))
            def _():
                there = pl.ds(pl.multiple_of((turn - 1) * tall, 16), tall)
                pltpu.make_async_copy(other_g.at[sec, here], rest_out.at[there], out_sem.at[1, index]).start()

    def sent():
        for index in range(4 * width // tall):
            here = pl.ds(0, tall)
            pltpu.make_async_copy(own_g.at[0, here], own_out.at[here], out_sem.at[0, index]).wait()
            pltpu.make_async_copy(other_g.at[0, here], near_out, out_sem.at[1, index]).wait()

    dims = (micro, length, width)

    def arrived(sec):
        for i, ref in enumerate(own_w):
            pltpu.make_async_copy(ref, w.at[sec, pl.ds(0, ref.shape[0])], in_sem.at[sec, i]).wait()

    live_copy.wait()
    x_copy.wait()
    arrived(0)
    forward(0, *dims, live_ref, x_ref, w, q_t, k, v, tr, p, mixed_t, xhat, rstd, hid)
    arrived(1)
    forward(1, *dims, live_ref, hid, w, q_t, k, v, tr, p, mixed_t, xhat, rstd, None)
    g_copy.wait()
    pieces = []
    for seq in range(micro):
        pos = lax.broadcasted_iota(jnp.int32, (length, width), 0)
        piece = g_ref[seq * length : (seq + 1) * length].astype(F32)
        pieces.append(jnp.where(pos < live_ref[0, seq], piece, 0.0))
    grad = jnp.concatenate(pieces, axis=0)
    back = backward(1, *dims, grad, hid, w, q_t, k, v, tr, p, mixed_t, xhat, rstd, g_t, dq_t, dk, dv, emit, None)
    send(1, (0, 1, 2, 3))
    backward(0, *dims, back.astype(F32), x_ref, w, q_t, k, v, tr, p, mixed_t, xhat, rstd, g_t, dq_t, dk, dv, emit, send)
    send(0, (2,))
    sent()


def run_layers(live, x, target, own, other, places, rows, count, micro, length, width):
    tokens = micro * length
    heads = width // HEAD
    hbm = pl.BlockSpec(memory_space=pl.ANY)
    far = pl.BlockSpec(memory_space=pltpu.HBM)
    first = rows if rows else width
    return pl.pallas_call(
        functools.partial(layers, micro, length, width, rows, count, places),
        out_shape=(
            jax.ShapeDtypeStruct((4 * width, width), F32),
            jax.ShapeDtypeStruct((first, width), BF16),
            jax.ShapeDtypeStruct((4 * width - first, width), BF16),
        ),
        in_specs=[far, far, hbm] + [hbm] * (2 * len(own)),
        out_specs=(hbm, hbm, hbm),
        scratch_shapes=[
            pltpu.SMEM((1, micro), jnp.int32),
            pltpu.VMEM((tokens, width), BF16),
            pltpu.VMEM((tokens, width), BF16),
            pltpu.VMEM((2, 4 * width, width), BF16),
            pltpu.VMEM((2, 4 * width, width), F32),
            pltpu.VMEM((2, 4 * width, width), BF16),
            pltpu.VMEM((tokens, width), BF16),
            pltpu.VMEM((2, width, tokens), BF16),
            pltpu.VMEM((2, tokens, width), BF16),
            pltpu.VMEM((2, tokens, width), BF16),
            pltpu.VMEM((width, tokens), BF16),
            pltpu.VMEM((2, micro * heads, length, length), F32),
            pltpu.VMEM((2, width, tokens), F32),
            pltpu.VMEM((2, tokens, width), F32),
            pltpu.VMEM((2, tokens, PAIR), F32),
            pltpu.VMEM((width, tokens), BF16),
            pltpu.VMEM((width, tokens), BF16),
            pltpu.VMEM((tokens, width), BF16),
            pltpu.VMEM((tokens, width), BF16),
            pltpu.SemaphoreType.DMA((2, len(own))),
            pltpu.SemaphoreType.DMA((2, 4 * width // first)),
            pltpu.SemaphoreType.DMA((3,)),
        ],
        compiler_params=pltpu.CompilerParams(vmem_limit_bytes=40 * 1024 * 1024),
    )(live, x, target, *own, *other)


def swapped(value):
    return lax.ppermute(value, "pipe", [(0, 1), (1, 0)])


def ring_order(count):
    return list(range(0, count, 2)) + list(range(count - 1, 0, -2))


def on_device(inputs, out_grad, lengths, master, moment_first, moment_second):
    count = lax.axis_size("dp")
    weights = master[0]
    rows, width = weights.shape
    micro, length = inputs.shape[1:3]
    ringed = count == 8 and rows % 32 == 0 and width % rows == 0
    ring = ring_order(count)
    onward = [(ring[i], ring[(i + 1) % count]) for i in range(count)]
    backward_way = [(b, a) for a, b in onward]

    def ahead(value):
        return lax.ppermute(value, "dp", onward)

    def behind(value):
        return lax.ppermute(value, "dp", backward_way)

    mine = weights.astype(BF16)
    target = out_grad[0].reshape(micro * length, width)
    x = inputs[0].reshape(micro * length, width)
    half = rows // 2
    if ringed:
        own = [mine]
        places = [(0, 0)]
        fore, aft = mine, mine
        beside = [target, mine]
        crossed = []
        for step in range(1, count // 2 + 1):
            last = step == count // 2
            if step > 1:
                fore, one = lax.optimization_barrier((fore, swapped(beside[0])))
                aft, two = lax.optimization_barrier((aft, swapped(beside[1])))
                crossed += [one, two]
                beside = [own[-2], own[-1]]
            fore, aft = ahead(fore[:half] if last else fore), behind(aft[half:] if last else aft)
            own += [fore, aft]
            places += [(count - step, 0), (step, half if last else 0)]
        crossed += [swapped(value) for value in own[-4:]]
        target, other = crossed[0], crossed[1:]
    else:
        own = [lax.all_gather(mine, "dp", axis=0, tiled=True)]
        places = [(0, 0)]
        target, other = swapped(target), [swapped(own[0])]
    own_g, near_g, rest_g = run_layers(
        lengths, x, target, own, other, places, rows if ringed else 0, count, micro, length, width
    )
    near_g = swapped(near_g)
    if ringed:
        mid = count // 2
        near = (own_g[:rows] + near_g.astype(F32)).astype(BF16)
        rest_g, near = lax.optimization_barrier((rest_g, near))
        fore, aft = ahead(near[:half]), behind(near[half:])
        rest_g = swapped(rest_g)

        def block(index):
            at = (index + mid) % count * rows
            return own_g[at : at + rows] + rest_g[at - rows : at].astype(F32)

        up, down = block(mid - 1), block(mid + 1)
        fore = jnp.concatenate([up[:half] + fore.astype(F32), up[half:]], axis=0).astype(BF16)
        aft = jnp.concatenate([down[:half], down[half:] + aft.astype(F32)], axis=0).astype(BF16)
        for step in range(mid - 2, -1, -1):
            fore, aft = lax.optimization_barrier((fore, aft))
            fore, aft = ahead(fore), behind(aft)
            if step:
                fore = (block(step) + fore.astype(F32)).astype(BF16)
                aft = (block(count - step) + aft.astype(F32)).astype(BF16)
        terms = ((own_g, mid * rows), (rest_g, (mid - 1) * rows), (fore, 0), (aft, 0))
    else:
        total = own_g + jnp.concatenate([near_g, swapped(rest_g)], axis=0).astype(F32)
        terms = ((lax.psum_scatter(total, "dp", scatter_dimension=0, tiled=True), 0),)
    new_first, new_second, update, squares = run_moments(weights, moment_first[0], moment_second[0], terms)
    if ringed:
        hop = 1
        while 2 * hop < count:
            squares = squares + lax.ppermute(squares, "dp", [(i, i ^ hop) for i in range(count)])
            hop *= 2
        pair = (squares, lax.ppermute(squares, "dp", [(i, i ^ hop) for i in range(count)]))
    else:
        pair = (lax.psum(squares, "dp"),)
    new_master = run_master(weights, update, pair)
    return (new_master[None], new_first[None], new_second[None])


def moments(starts, w_in, first_in, second_in, *refs):
    count = len(starts)
    terms_in, refs = refs[:count], refs[count:]
    outs_out, squares_out, refs = refs[:3], refs[3], refs[4:]
    weights, first, second = refs[:3]
    terms, outs, squares, in_sem, out_sem = refs[3 : 3 + count], refs[3 + count : 6 + count], *refs[6 + count :]
    rows, width = weights.shape
    loads = [
        pltpu.make_async_copy(src, dst, in_sem.at[i])
        for i, (src, dst) in enumerate(
            [(src.at[pl.ds(at, rows)], dst) for src, at, dst in zip(terms_in, starts, terms)]
            + [(w_in, weights), (first_in, first), (second_in, second)]
        )
    ]
    for copy in loads:
        copy.start()
    for copy in loads:
        copy.wait()
    pieces = CUTS if rows % (CUTS * 8) == 0 else 1
    tall = rows // pieces
    sums = [jnp.zeros((8, 128), F32), jnp.zeros((8, 128), F32)]
    stores = []
    for piece in range(pieces):
        here = slice(piece * tall, (piece + 1) * tall)
        grad = terms[0][here]
        for term in terms[1:]:
            grad = grad + term[here].astype(F32)
        new_first = 0.9 * first[here] + 0.1 * grad
        new_second = 0.999 * second[here] + 0.001 * grad * grad
        corrected = new_first * (1.0 / (1.0 - 0.9**STEP))
        spread = new_second * (1.0 / (1.0 - 0.999**STEP))
        update = corrected / (jnp.sqrt(spread) + 1e-06) + 0.05 * weights[here]
        for index, value in enumerate((new_first, new_second, update)):
            outs[index][here] = value
            copy = pltpu.make_async_copy(outs[index].at[here], outs_out[index].at[here], out_sem.at[index, piece])
            copy.start()
            stores.append(copy)
        for index, value in enumerate((weights[here], update)):
            square = jnp.sum((value * value).reshape(tall // 8, 8, width), axis=0)
            for start in range(0, width, 128):
                sums[index] = sums[index] + square[:, start : start + 128]
    squares[...] = jnp.concatenate(sums, axis=0)
    copy = pltpu.make_async_copy(squares, squares_out, in_sem.at[0])
    copy.start()
    for store in stores + [copy]:
        store.wait()


def run_moments(weights, first, second, terms):
    free = pl.BlockSpec(memory_space=pl.ANY)
    rows, width = weights.shape
    same = jax.ShapeDtypeStruct(weights.shape, F32)
    return pl.pallas_call(
        functools.partial(moments, tuple(at for _, at in terms)),
        out_shape=(same, same, same, jax.ShapeDtypeStruct((16, 128), F32)),
        in_specs=[free] * (3 + len(terms)),
        out_specs=(free,) * 4,
        scratch_shapes=[pltpu.VMEM((rows, width), F32)] * 3
        + [pltpu.VMEM((rows, width), term.dtype) for term, _ in terms]
        + [pltpu.VMEM((rows, width), F32)] * 3
        + [
            pltpu.VMEM((16, 128), F32),
            pltpu.SemaphoreType.DMA((3 + len(terms),)),
            pltpu.SemaphoreType.DMA((3, CUTS)),
        ],
        compiler_params=pltpu.CompilerParams(vmem_limit_bytes=12 * 1024 * 1024),
    )(weights, first, second, *[term for term, _ in terms])


def master_step(w_in, update_in, *refs):
    count = (len(refs) - 5) // 2
    squares_in, out, refs = refs[:count], refs[count], refs[count + 1 :]
    weights, update, squares, in_sem, out_sem = refs[0], refs[1], refs[2 : 2 + count], *refs[2 + count :]
    loads = [
        pltpu.make_async_copy(src, dst, in_sem.at[i])
        for i, (src, dst) in enumerate([*zip(squares_in, squares), (w_in, weights), (update_in, update)])
    ]
    for copy in loads:
        copy.start()
    for copy in loads:
        copy.wait()
    total = squares[0][...]
    for more in squares[1:]:
        total = total + more[...]
    weight_sq = jnp.sum(total[:8], axis=(0, 1), keepdims=True)
    update_sq = jnp.sum(total[8:], axis=(0, 1), keepdims=True)
    trust = jnp.sqrt(weight_sq) / (jnp.sqrt(update_sq) + 1e-06)
    rows, width = weights.shape
    pieces = CUTS if rows % (CUTS * 8) == 0 else 1
    stores = []
    for piece in range(pieces):
        here = slice(piece * rows // pieces, (piece + 1) * rows // pieces)
        update[here] = weights[here] - 0.05 * trust * update[here]
        copy = pltpu.make_async_copy(update.at[here], out.at[here], out_sem.at[piece])
        copy.start()
        stores.append(copy)
    for copy in stores:
        copy.wait()


def run_master(weights, update, pair):
    free = pl.BlockSpec(memory_space=pl.ANY)
    rows, width = weights.shape
    return pl.pallas_call(
        master_step,
        out_shape=jax.ShapeDtypeStruct(weights.shape, F32),
        in_specs=[free] * (2 + len(pair)),
        out_specs=free,
        scratch_shapes=[pltpu.VMEM((rows, width), F32)] * 2
        + [pltpu.VMEM((16, 128), F32)] * len(pair)
        + [pltpu.SemaphoreType.DMA((2 + len(pair),)), pltpu.SemaphoreType.DMA((CUTS,))],
        compiler_params=pltpu.CompilerParams(vmem_limit_bytes=6 * 1024 * 1024),
    )(weights, update, *pair)


def solution(mesh):
    rows = P("pipe", ("groups", "dp"), None)
    in_specs = (
        P("pipe", ("groups", "dp"), None, None),
        P("pipe", ("groups", "dp"), None, None),
        P("pipe", ("groups", "dp")),
        rows,
        rows,
        rows,
    )
    return jax.shard_map(
        on_device, mesh=mesh, in_specs=in_specs, out_specs=(rows, rows, rows), check_vma=False
    )
```

```python
import functools

import jax
import jax.numpy as jnp
from jax import lax
from jax.experimental import pallas as pl
from jax.experimental.pallas import tpu as pltpu
from jax.sharding import PartitionSpec as P

HEAD = 64
PAIR = 128
AHEAD = 4
CUTS = 4
STEP = 10
F32 = jnp.float32
BF16 = jnp.bfloat16


def dot(a, b):
    return lax.dot_general(a, b, (((1,), (0,)), ((), ())), preferred_element_type=F32)


def dot_nt(a, b):
    return lax.dot_general(a, b, (((1,), (1,)), ((), ())), preferred_element_type=F32)


def padded(part, half):
    zero = jnp.zeros_like(part)
    return jnp.concatenate([part, zero] if half == 0 else [zero, part], axis=0)


def forward(sec, micro, length, width, live_ref, x_ref, w, q_t, k, v, tr, p, mixed_t, xhat, rstd, h_ref):
    factor = width ** (-0.5)
    x2 = x_ref[...]
    queries = (dot(x2, w[sec, 0:width]) * factor).astype(BF16) * jnp.asarray(HEAD ** (-0.5), BF16)
    q_t[sec] = queries.T
    k[sec] = (dot(x2, w[sec, width : 2 * width]) * factor).astype(BF16)
    values = (dot(x2, w[sec, 2 * width : 3 * width]) * factor).astype(BF16)
    v[sec] = values
    tr[...] = values.T
    lane = lax.broadcasted_iota(jnp.int32, (length, PAIR), 1)
    spot = lax.broadcasted_iota(jnp.int32, (length, PAIR), 0)
    first = (lax.broadcasted_iota(jnp.int32, (HEAD, length), 0) == 0).astype(F32).astype(BF16)
    heads = width // HEAD
    bias = [jnp.where(spot < live_ref[0, seq], 0.0, -1e30).astype(BF16) for seq in range(micro)]

    def scores(index):
        seq, head = divmod(index, heads)
        rows = slice(seq * length, (seq + 1) * length)
        kp = k[sec, rows, (head // 2) * PAIR : (head // 2 + 1) * PAIR]
        k_ext = jnp.where(lane == (0 if head % 2 else HEAD), bias[seq], kp)
        qh = q_t[sec, head * HEAD : (head + 1) * HEAD, rows]
        return dot(k_ext, jnp.concatenate([first, qh] if head % 2 else [qh, first], axis=0))

    waiting = [scores(index) for index in range(AHEAD)]
    for index in range(micro * heads):
        if index + AHEAD < micro * heads:
            waiting.append(scores(index + AHEAD))
        score = waiting.pop(0)
        seq, head = divmod(index, heads)
        rows = slice(seq * length, (seq + 1) * length)
        feats = slice(head * HEAD, (head + 1) * HEAD)
        expo = jnp.exp(score - jnp.max(score, axis=0, keepdims=True))
        prob = expo * (1.0 / jnp.sum(expo, axis=0, keepdims=True))
        p[sec, index] = prob
        mixed_t[sec, feats, rows] = dot(tr[feats, rows], prob.astype(BF16))
    mixed = mixed_t[sec].astype(BF16).T
    resid = x2.astype(F32) + dot(mixed, w[sec, 3 * width : 4 * width]) * factor
    centre = resid - jnp.mean(resid, axis=-1, keepdims=True)
    scale = lax.rsqrt(jnp.mean(centre * centre, axis=-1, keepdims=True) + 1e-05)
    normed = centre * scale
    xhat[sec] = normed
    rstd[sec] = jnp.broadcast_to(scale, rstd.shape[1:])
    if h_ref is not None:
        h_ref[...] = normed.astype(BF16)


def backward(sec, micro, length, width, grad, x_ref, w, q_t, k, v, tr, p, mixed_t, xhat, rstd, g_t, dq_t, dk, dv, emit, send):
    factor = width ** (-0.5)
    normed = xhat[sec]
    dres = rstd[sec][:, :1] * (
        grad
        - jnp.mean(grad, axis=-1, keepdims=True)
        - normed * jnp.mean(grad * normed, axis=-1, keepdims=True)
    )
    da = dres.astype(BF16)
    emit(sec, 3, dot(mixed_t[sec].astype(BF16), da) * factor)
    g_t[...] = (dot_nt(w[sec, 3 * width : 4 * width], da) * factor).astype(BF16)
    tr[...] = k[sec].T
    heads = width // HEAD

    def spread(index):
        seq, head = divmod(index, heads)
        rows = slice(seq * length, (seq + 1) * length)
        g_ext = padded(g_t[head * HEAD : (head + 1) * HEAD, rows], head % 2)
        return g_ext, dot(v[sec, rows, (head // 2) * PAIR : (head // 2 + 1) * PAIR], g_ext)

    waiting = [spread(index) for index in range(AHEAD)]
    for index in range(micro * heads):
        if index + AHEAD < micro * heads:
            waiting.append(spread(index + AHEAD))
        g_ext, dp = waiting.pop(0)
        seq, head = divmod(index, heads)
        rows = slice(seq * length, (seq + 1) * length)
        feats = slice(head * HEAD, (head + 1) * HEAD)
        q_ext = padded(q_t[sec, feats, rows], head % 2)
        delta = jnp.sum(mixed_t[sec, feats, rows] * g_t[feats, rows].astype(F32), axis=0, keepdims=True)
        prob = p[sec, index]
        ds = (prob * (dp - delta)).astype(BF16)
        gv_part = dot_nt(prob.astype(BF16), g_ext)
        gk_part = dot_nt(ds, q_ext)
        dq_t[feats, rows] = (dot(tr[feats, rows], ds) * HEAD ** (-0.5)).astype(BF16)
        if head % 2 == 0:
            gv, gk = gv_part, gk_part
        else:
            lanes = slice((head // 2) * PAIR, (head // 2 + 1) * PAIR)
            dv[rows, lanes] = (gv + gv_part).astype(BF16)
            dk[rows, lanes] = (gk + gk_part).astype(BF16)
    if send is not None:
        send(sec, (3,))
    dq = dq_t[...].T
    x_t = x_ref[...].T
    emit(sec, 0, dot(x_t, dq) * factor)
    emit(sec, 1, dot(x_t, dk[...]) * factor)
    if send is not None:
        send(sec, (0, 1))
    emit(sec, 2, dot(x_t, dv[...]) * factor)
    if send is not None:
        return None
    back = dot_nt(dq, w[sec, 0:width])
    back += dot_nt(dk[...], w[sec, width : 2 * width])
    back += dot_nt(dv[...], w[sec, 2 * width : 3 * width])
    return (dres + back * factor).astype(BF16)


def ring_spot(index, count):
    return jnp.where(index % 2 == 0, index // 2, count - 1 - index // 2)


def ring_index(spot, count):
    return jnp.where(spot < count // 2, 2 * spot, 2 * (count - 1 - spot) + 1)


def layers(micro, length, width, rows, count, plan, groups, live_in, x_in, g_in, *refs):
    sizes = [len(part) for part in plan]
    size = sum(sizes)
    own_w = [(refs[i], piece) for i, part in enumerate(plan[0]) for piece in part]
    other_w = [(refs[sizes[0] + i], piece) for i, part in enumerate(plan[1]) for piece in part]
    own_out, other_outs = refs[size], refs[size + 1 : size + 1 + len(groups)]
    (live_ref, x_ref, g_ref, w, own_g, other_g, hid, q_t, k, v, tr, p, mixed_t, xhat, rstd, g_t, dq_t, dk, dv, in_sem, out_sem, act_sem) = refs[size + 1 + len(groups) :]
    side = lax.axis_index("pipe")
    me = ring_spot(lax.axis_index("dp"), count)
    block = rows if rows else 4 * width
    live_copy = pltpu.make_async_copy(live_in, live_ref, act_sem.at[2])
    x_copy = pltpu.make_async_copy(x_in, x_ref, act_sem.at[0])
    g_copy = pltpu.make_async_copy(g_in, g_ref, act_sem.at[1])
    live_copy.start()
    x_copy.start()
    def load(sec, group):
        for i, (ref, (slot, shift, start, tall)) in enumerate(group):
            at = pl.multiple_of(ring_index((me + slot) % count, count) * rows + shift, 16) if rows else 0
            there = w.at[sec, pl.ds(at, tall)]
            pltpu.make_async_copy(ref.at[pl.ds(start, tall)], there, in_sem.at[sec, i]).start()

    @pl.when(side == 0)
    def _():
        load(0, own_w)
        load(1, other_w)

    @pl.when(side != 0)
    def _():
        load(0, other_w)
        load(1, own_w)

    tall = rows if rows else width
    g_copy.start()

    starts = [sum(groups[:i]) for i in range(len(groups))]

    def turn_of(index):
        if not rows:
            return index
        away = (ring_spot(jnp.int32(index), count) - me + count) % count - count // 2
        return jnp.where(away < 0, -2 * away - 1, 2 * away)

    def emit(sec, part, value):
        for b in range(width // tall):
            here = pl.ds(pl.multiple_of(turn_of(part * (width // tall) + b) * tall, 16), tall)
            piece = value[b * tall : (b + 1) * tall]
            own_g[sec, here] = piece
            other_g[sec, here] = piece.astype(BF16)

    def send(sec, parts):
        for index in [part * (width // tall) + b for part in parts for b in range(width // tall)]:
            turn = turn_of(index)
            here = pl.ds(pl.multiple_of(turn * tall, 16), tall)

            @pl.when(side == sec)
            def _():
                pltpu.make_async_copy(own_g.at[sec, here], own_out.at[here], out_sem.at[0, index]).start()

            for start, blocks, out in zip(starts, groups, other_outs):

                @pl.when((side != sec) & (turn >= start) & (turn < start + blocks))
                def _():
                    there = pl.ds(pl.multiple_of((turn - start) * tall, 16), tall)
                    pltpu.make_async_copy(other_g.at[sec, here], out.at[there], out_sem.at[1, index]).start()

    def sent():
        for index in range(4 * width // tall):
            here = pl.ds(0, tall)
            pltpu.make_async_copy(own_g.at[0, here], own_out.at[here], out_sem.at[0, index]).wait()
            pltpu.make_async_copy(other_g.at[0, here], other_outs[0], out_sem.at[1, index]).wait()

    dims = (micro, length, width)

    def arrived(sec):
        for i, (ref, (slot, shift, start, tall)) in enumerate(own_w):
            there = w.at[sec, pl.ds(0, tall)]
            pltpu.make_async_copy(ref.at[pl.ds(start, tall)], there, in_sem.at[sec, i]).wait()

    live_copy.wait()
    x_copy.wait()
    arrived(0)
    forward(0, *dims, live_ref, x_ref, w, q_t, k, v, tr, p, mixed_t, xhat, rstd, hid)
    arrived(1)
    forward(1, *dims, live_ref, hid, w, q_t, k, v, tr, p, mixed_t, xhat, rstd, None)
    g_copy.wait()
    pieces = []
    for seq in range(micro):
        pos = lax.broadcasted_iota(jnp.int32, (length, width), 0)
        piece = g_ref[seq * length : (seq + 1) * length].astype(F32)
        pieces.append(jnp.where(pos < live_ref[0, seq], piece, 0.0))
    grad = jnp.concatenate(pieces, axis=0)
    back = backward(1, *dims, grad, hid, w, q_t, k, v, tr, p, mixed_t, xhat, rstd, g_t, dq_t, dk, dv, emit, None)
    send(1, (0, 1, 2, 3))
    backward(0, *dims, back.astype(F32), x_ref, w, q_t, k, v, tr, p, mixed_t, xhat, rstd, g_t, dq_t, dk, dv, emit, send)
    send(0, (2,))
    sent()


def run_layers(live, x, target, own, other, plan, groups, rows, count, micro, length, width):
    tokens = micro * length
    heads = width // HEAD
    hbm = pl.BlockSpec(memory_space=pl.ANY)
    far = pl.BlockSpec(memory_space=pltpu.HBM)
    first = rows if rows else width
    return pl.pallas_call(
        functools.partial(layers, micro, length, width, rows, count, plan, groups),
        out_shape=(
            jax.ShapeDtypeStruct((4 * width, width), F32),
            *[jax.ShapeDtypeStruct((blocks * first, width), BF16) for blocks in groups],
        ),
        in_specs=[far, far, hbm] + [hbm] * (len(own) + len(other)),
        out_specs=(hbm,) * (1 + len(groups)),
        scratch_shapes=[
            pltpu.SMEM((1, micro), jnp.int32),
            pltpu.VMEM((tokens, width), BF16),
            pltpu.VMEM((tokens, width), BF16),
            pltpu.VMEM((2, 4 * width, width), BF16),
            pltpu.VMEM((2, 4 * width, width), F32),
            pltpu.VMEM((2, 4 * width, width), BF16),
            pltpu.VMEM((tokens, width), BF16),
            pltpu.VMEM((2, width, tokens), BF16),
            pltpu.VMEM((2, tokens, width), BF16),
            pltpu.VMEM((2, tokens, width), BF16),
            pltpu.VMEM((width, tokens), BF16),
            pltpu.VMEM((2, micro * heads, length, length), F32),
            pltpu.VMEM((2, width, tokens), F32),
            pltpu.VMEM((2, tokens, width), F32),
            pltpu.VMEM((2, tokens, PAIR), F32),
            pltpu.VMEM((width, tokens), BF16),
            pltpu.VMEM((width, tokens), BF16),
            pltpu.VMEM((tokens, width), BF16),
            pltpu.VMEM((tokens, width), BF16),
            pltpu.SemaphoreType.DMA((2, sum(len(part) for part in plan[0]))),
            pltpu.SemaphoreType.DMA((2, 4 * width // first)),
            pltpu.SemaphoreType.DMA((3,)),
        ],
        compiler_params=pltpu.CompilerParams(vmem_limit_bytes=40 * 1024 * 1024),
    )(pltpu.with_memory_space_constraint(live, pltpu.HBM), pltpu.with_memory_space_constraint(x, pltpu.HBM), target, *own, *other)


def swapped(value):
    return lax.ppermute(value, "pipe", [(0, 1), (1, 0)])


def ring_order(count):
    return list(range(0, count, 2)) + list(range(count - 1, 0, -2))


def on_device(inputs, out_grad, lengths, master, moment_first, moment_second):
    count = lax.axis_size("dp")
    weights = master[0]
    rows, width = weights.shape
    micro, length = inputs.shape[1:3]
    ringed = count == 8 and rows % 32 == 0 and width % rows == 0
    ring = ring_order(count)
    onward = [(ring[i], ring[(i + 1) % count]) for i in range(count)]
    backward_way = [(b, a) for a, b in onward]

    def ahead(value):
        return lax.ppermute(value, "dp", onward)

    def behind(value):
        return lax.ppermute(value, "dp", backward_way)

    mine = weights.astype(BF16)
    target = out_grad[0].reshape(micro * length, width)
    x = inputs[0].reshape(micro * length, width)
    half = rows // 2
    mid = count // 2
    if ringed:
        own, plan_own = [mine], [((0, 0, 0, rows),)]
        fore, aft = mine, mine
        target, other, plan_other = swapped(target), [swapped(mine)], [((0, 0, 0, rows),)]
        for step in range(1, mid + 1):
            last = step == mid
            size = half if last else rows
            fore, aft = ahead(fore[:half] if last else fore), behind(aft[half:] if last else aft)
            own += [fore, aft]
            places = ((count - step, 0), (step, half if last else 0))
            plan_own += [((*place, 0, size),) for place in places]
            if last:
                other += [swapped(fore), swapped(aft)]
                plan_other += [((*place, 0, size),) for place in places]
            else:
                other.append(swapped(jnp.concatenate([fore, aft], axis=0)))
                plan_other.append(tuple((*place, i * size, size) for i, place in enumerate(places)))
    else:
        own = [lax.all_gather(mine, "dp", axis=0, tiled=True)]
        target, other = swapped(target), [swapped(own[0])]
        plan_own = plan_other = [((0, 0, 0, 4 * width),)]
    plan = (tuple(plan_own), tuple(plan_other))
    groups = (1, count - 1) if ringed else (4,)
    own_g, *far_g = run_layers(
        lengths, x, target, own, other, plan, groups, rows if ringed else 0, count, micro, length, width
    )
    far_g[0] = swapped(far_g[0])
    if ringed:
        near = (own_g[:rows] + far_g[0].astype(F32)).astype(BF16)
        far_g[1], near = lax.optimization_barrier((far_g[1], near))
        fore, aft = ahead(near[:half]), behind(near[half:])
        far = swapped(far_g[1])

        def block(index):
            at = index * rows
            return own_g[at : at + rows] + far[at - rows : at].astype(F32)

        for step in range(1, mid):
            up, down = block(2 * step - 1), block(2 * step)
            if step == 1:
                up = jnp.concatenate([up[:half] + fore.astype(F32), up[half:]], axis=0)
                down = jnp.concatenate([down[:half], down[half:] + aft.astype(F32)], axis=0)
            else:
                up, down = up + fore.astype(F32), down + aft.astype(F32)
            fore, aft = lax.optimization_barrier((up.astype(BF16), down.astype(BF16)))
            fore, aft = ahead(fore), behind(aft)
        terms = ((own_g, (count - 1) * rows), (far, (count - 2) * rows), (fore, 0), (aft, 0))
    else:
        total = own_g + far_g[0].astype(F32)
        terms = ((lax.psum_scatter(total, "dp", scatter_dimension=0, tiled=True), 0),)
    new_first, new_second, update, squares = run_moments(weights, moment_first[0], moment_second[0], terms)
    if ringed:
        hop = 1
        while 2 * hop < count:
            squares = squares + lax.ppermute(squares, "dp", [(i, i ^ hop) for i in range(count)])
            hop *= 2
        pair = (squares, lax.ppermute(squares, "dp", [(i, i ^ hop) for i in range(count)]))
    else:
        pair = (lax.psum(squares, "dp"),)
    new_master = run_master(weights, update, pair)
    return (new_master[None], new_first[None], new_second[None])


def moments(starts, w_in, first_in, second_in, *refs):
    count = len(starts)
    terms_in, refs = refs[:count], refs[count:]
    outs_out, squares_out, refs = refs[:3], refs[3], refs[4:]
    weights, first, second = refs[:3]
    terms, outs, squares, in_sem, out_sem = refs[3 : 3 + count], refs[3 + count : 6 + count], *refs[6 + count :]
    rows, width = weights.shape
    loads = [
        pltpu.make_async_copy(src, dst, in_sem.at[i])
        for i, (src, dst) in enumerate(
            [(src.at[pl.ds(at, rows)], dst) for src, at, dst in zip(terms_in, starts, terms)]
            + [(w_in, weights), (first_in, first), (second_in, second)]
        )
    ]
    for copy in loads:
        copy.start()
    for copy in loads:
        copy.wait()
    pieces = CUTS if rows % (CUTS * 8) == 0 else 1
    tall = rows // pieces
    sums = [jnp.zeros((8, 128), F32), jnp.zeros((8, 128), F32)]
    stores = []
    for piece in range(pieces):
        here = slice(piece * tall, (piece + 1) * tall)
        grad = terms[0][here]
        for term in terms[1:]:
            grad = grad + term[here].astype(F32)
        new_first = 0.9 * first[here] + 0.1 * grad
        new_second = 0.999 * second[here] + 0.001 * grad * grad
        corrected = new_first * (1.0 / (1.0 - 0.9**STEP))
        spread = new_second * (1.0 / (1.0 - 0.999**STEP))
        update = corrected / (jnp.sqrt(spread) + 1e-06) + 0.05 * weights[here]
        for index, value in enumerate((new_first, new_second, update)):
            outs[index][here] = value
            copy = pltpu.make_async_copy(outs[index].at[here], outs_out[index].at[here], out_sem.at[index, piece])
            copy.start()
            stores.append(copy)
        for index, value in enumerate((weights[here], update)):
            square = jnp.sum((value * value).reshape(tall // 8, 8, width), axis=0)
            for start in range(0, width, 128):
                sums[index] = sums[index] + square[:, start : start + 128]
    squares[...] = jnp.concatenate(sums, axis=0)
    copy = pltpu.make_async_copy(squares, squares_out, in_sem.at[0])
    copy.start()
    for store in stores + [copy]:
        store.wait()


def run_moments(weights, first, second, terms):
    free = pl.BlockSpec(memory_space=pl.ANY)
    rows, width = weights.shape
    same = jax.ShapeDtypeStruct(weights.shape, F32)
    return pl.pallas_call(
        functools.partial(moments, tuple(at for _, at in terms)),
        out_shape=(same, same, same, jax.ShapeDtypeStruct((16, 128), F32)),
        in_specs=[free] * (3 + len(terms)),
        out_specs=(free,) * 4,
        scratch_shapes=[pltpu.VMEM((rows, width), F32)] * 3
        + [pltpu.VMEM((rows, width), term.dtype) for term, _ in terms]
        + [pltpu.VMEM((rows, width), F32)] * 3
        + [
            pltpu.VMEM((16, 128), F32),
            pltpu.SemaphoreType.DMA((3 + len(terms),)),
            pltpu.SemaphoreType.DMA((3, CUTS)),
        ],
        compiler_params=pltpu.CompilerParams(vmem_limit_bytes=12 * 1024 * 1024),
    )(weights, first, second, *[term for term, _ in terms])


def master_step(w_in, update_in, *refs):
    count = (len(refs) - 5) // 2
    squares_in, out, refs = refs[:count], refs[count], refs[count + 1 :]
    weights, update, squares, in_sem, out_sem = refs[0], refs[1], refs[2 : 2 + count], *refs[2 + count :]
    loads = [
        pltpu.make_async_copy(src, dst, in_sem.at[i])
        for i, (src, dst) in enumerate([*zip(squares_in, squares), (w_in, weights), (update_in, update)])
    ]
    for copy in loads:
        copy.start()
    for copy in loads:
        copy.wait()
    total = squares[0][...]
    for more in squares[1:]:
        total = total + more[...]
    weight_sq = jnp.sum(total[:8], axis=(0, 1), keepdims=True)
    update_sq = jnp.sum(total[8:], axis=(0, 1), keepdims=True)
    trust = jnp.sqrt(weight_sq) / (jnp.sqrt(update_sq) + 1e-06)
    rows, width = weights.shape
    pieces = CUTS if rows % (CUTS * 8) == 0 else 1
    stores = []
    for piece in range(pieces):
        here = slice(piece * rows // pieces, (piece + 1) * rows // pieces)
        update[here] = weights[here] - 0.05 * trust * update[here]
        copy = pltpu.make_async_copy(update.at[here], out.at[here], out_sem.at[piece])
        copy.start()
        stores.append(copy)
    for copy in stores:
        copy.wait()


def run_master(weights, update, pair):
    free = pl.BlockSpec(memory_space=pl.ANY)
    rows, width = weights.shape
    return pl.pallas_call(
        master_step,
        out_shape=jax.ShapeDtypeStruct(weights.shape, F32),
        in_specs=[free] * (2 + len(pair)),
        out_specs=free,
        scratch_shapes=[pltpu.VMEM((rows, width), F32)] * 2
        + [pltpu.VMEM((16, 128), F32)] * len(pair)
        + [pltpu.SemaphoreType.DMA((2 + len(pair),)), pltpu.SemaphoreType.DMA((CUTS,))],
        compiler_params=pltpu.CompilerParams(vmem_limit_bytes=6 * 1024 * 1024),
    )(weights, update, *pair)


def solution(mesh):
    rows = P("pipe", ("groups", "dp"), None)
    in_specs = (
        P("pipe", ("groups", "dp"), None, None),
        P("pipe", ("groups", "dp"), None, None),
        P("pipe", ("groups", "dp")),
        rows,
        rows,
        rows,
    )
    return jax.shard_map(
        on_device, mesh=mesh, in_specs=in_specs, out_specs=(rows, rows, rows), check_vma=False
    )
```

```python
import functools

import jax
import jax.numpy as jnp
from jax import lax
from jax.experimental import pallas as pl
from jax.experimental.pallas import tpu as pltpu
from jax.sharding import PartitionSpec as P

HEAD = 64
PAIR = 128
AHEAD = 6
CUTS = 1
STEP = 10
F32 = jnp.float32
BF16 = jnp.bfloat16


def dot(a, b):
    return lax.dot_general(a, b, (((1,), (0,)), ((), ())), preferred_element_type=F32)


def dot_nt(a, b):
    return lax.dot_general(a, b, (((1,), (1,)), ((), ())), preferred_element_type=F32)


def padded(part, half):
    zero = jnp.zeros_like(part)
    return jnp.concatenate([part, zero] if half == 0 else [zero, part], axis=0)


def forward(sec, micro, length, width, live_ref, x_ref, w, q_t, k, v, tr, p, mixed_t, xhat, rstd, h_ref):
    factor = width ** (-0.5)
    x2 = x_ref[...]
    queries = (dot(x2, w[sec, 0:width]) * factor).astype(BF16) * jnp.asarray(HEAD ** (-0.5), BF16)
    q_t[sec] = queries.T
    k[sec] = (dot(x2, w[sec, width : 2 * width]) * factor).astype(BF16)
    values = (dot(x2, w[sec, 2 * width : 3 * width]) * factor).astype(BF16)
    v[sec] = values
    tr[...] = values.T
    lane = lax.broadcasted_iota(jnp.int32, (length, PAIR), 1)
    spot = lax.broadcasted_iota(jnp.int32, (length, PAIR), 0)
    first = (lax.broadcasted_iota(jnp.int32, (HEAD, length), 0) == 0).astype(F32).astype(BF16)
    heads = width // HEAD
    bias = [jnp.where(spot < live_ref[0, seq], 0.0, -1e30).astype(BF16) for seq in range(micro)]

    def scores(index):
        seq, head = divmod(index, heads)
        rows = slice(seq * length, (seq + 1) * length)
        kp = k[sec, rows, (head // 2) * PAIR : (head // 2 + 1) * PAIR]
        k_ext = jnp.where(lane == (0 if head % 2 else HEAD), bias[seq], kp)
        qh = q_t[sec, head * HEAD : (head + 1) * HEAD, rows]
        return dot(k_ext, jnp.concatenate([first, qh] if head % 2 else [qh, first], axis=0))

    waiting = [scores(index) for index in range(AHEAD)]
    for index in range(micro * heads):
        if index + AHEAD < micro * heads:
            waiting.append(scores(index + AHEAD))
        score = waiting.pop(0)
        seq, head = divmod(index, heads)
        rows = slice(seq * length, (seq + 1) * length)
        feats = slice(head * HEAD, (head + 1) * HEAD)
        expo = jnp.exp(score - jnp.max(score, axis=0, keepdims=True))
        prob = expo * (1.0 / jnp.sum(expo, axis=0, keepdims=True))
        p[sec, index] = prob
        mixed_t[sec, feats, rows] = dot(tr[feats, rows], prob.astype(BF16))
    mixed = mixed_t[sec].astype(BF16).T
    resid = x2.astype(F32) + dot(mixed, w[sec, 3 * width : 4 * width]) * factor
    centre = resid - jnp.mean(resid, axis=-1, keepdims=True)
    scale = lax.rsqrt(jnp.mean(centre * centre, axis=-1, keepdims=True) + 1e-05)
    normed = centre * scale
    xhat[sec] = normed
    rstd[sec] = jnp.broadcast_to(scale, rstd.shape[1:])
    if h_ref is not None:
        h_ref[...] = normed.astype(BF16)


def backward(sec, micro, length, width, grad, x_ref, w, q_t, k, v, tr, p, mixed_t, xhat, rstd, g_t, dq_t, dk, dv, emit, send):
    factor = width ** (-0.5)
    normed = xhat[sec]
    dres = rstd[sec][:, :1] * (
        grad
        - jnp.mean(grad, axis=-1, keepdims=True)
        - normed * jnp.mean(grad * normed, axis=-1, keepdims=True)
    )
    da = dres.astype(BF16)
    emit(sec, 3, dot(mixed_t[sec].astype(BF16), da) * factor)
    g_t[...] = (dot_nt(w[sec, 3 * width : 4 * width], da) * factor).astype(BF16)
    tr[...] = k[sec].T
    heads = width // HEAD

    def spread(index):
        seq, head = divmod(index, heads)
        rows = slice(seq * length, (seq + 1) * length)
        g_ext = padded(g_t[head * HEAD : (head + 1) * HEAD, rows], head % 2)
        return g_ext, dot(v[sec, rows, (head // 2) * PAIR : (head // 2 + 1) * PAIR], g_ext)

    waiting = [spread(index) for index in range(AHEAD)]
    for index in range(micro * heads):
        if index + AHEAD < micro * heads:
            waiting.append(spread(index + AHEAD))
        g_ext, dp = waiting.pop(0)
        seq, head = divmod(index, heads)
        rows = slice(seq * length, (seq + 1) * length)
        feats = slice(head * HEAD, (head + 1) * HEAD)
        q_ext = padded(q_t[sec, feats, rows], head % 2)
        delta = jnp.sum(mixed_t[sec, feats, rows] * g_t[feats, rows].astype(F32), axis=0, keepdims=True)
        prob = p[sec, index]
        ds = (prob * (dp - delta)).astype(BF16)
        gv_part = dot_nt(prob.astype(BF16), g_ext)
        gk_part = dot_nt(ds, q_ext)
        dq_t[feats, rows] = (dot(tr[feats, rows], ds) * HEAD ** (-0.5)).astype(BF16)
        if head % 2 == 0:
            gv, gk = gv_part, gk_part
        else:
            lanes = slice((head // 2) * PAIR, (head // 2 + 1) * PAIR)
            dv[rows, lanes] = (gv + gv_part).astype(BF16)
            dk[rows, lanes] = (gk + gk_part).astype(BF16)
    if send is not None:
        send(sec, (3,))
    dq = dq_t[...].T
    x_t = x_ref[...].T
    emit(sec, 0, dot(x_t, dq) * factor)
    emit(sec, 1, dot(x_t, dk[...]) * factor)
    if send is not None:
        send(sec, (0, 1))
    emit(sec, 2, dot(x_t, dv[...]) * factor)
    if send is not None:
        return None
    back = dot_nt(dq, w[sec, 0:width])
    back += dot_nt(dk[...], w[sec, width : 2 * width])
    back += dot_nt(dv[...], w[sec, 2 * width : 3 * width])
    return (dres + back * factor).astype(BF16)


def ring_spot(index, count):
    return jnp.where(index % 2 == 0, index // 2, count - 1 - index // 2)


def ring_index(spot, count):
    return jnp.where(spot < count // 2, 2 * spot, 2 * (count - 1 - spot) + 1)


def layers(micro, length, width, rows, count, plan, groups, live_in, x_in, g_in, *refs):
    sizes = [len(part) for part in plan]
    size = sum(sizes)
    own_w = [(refs[i], piece) for i, part in enumerate(plan[0]) for piece in part]
    other_w = [(refs[sizes[0] + i], piece) for i, part in enumerate(plan[1]) for piece in part]
    own_out, other_outs = refs[size], refs[size + 1 : size + 1 + len(groups)]
    (live_ref, x_ref, g_ref, w, own_g, other_g, hid, q_t, k, v, tr, p, mixed_t, xhat, rstd, g_t, dq_t, dk, dv, in_sem, out_sem, act_sem) = refs[size + 1 + len(groups) :]
    side = lax.axis_index("pipe")
    me = ring_spot(lax.axis_index("dp"), count)
    block = rows if rows else 4 * width
    live_copy = pltpu.make_async_copy(live_in, live_ref, act_sem.at[2])
    x_copy = pltpu.make_async_copy(x_in, x_ref, act_sem.at[0])
    g_copy = pltpu.make_async_copy(g_in, g_ref, act_sem.at[1])
    live_copy.start()
    x_copy.start()
    def load(sec, group):
        for i, (ref, (slot, shift, start, tall)) in enumerate(group):
            at = pl.multiple_of(ring_index((me + slot) % count, count) * rows + shift, 16) if rows else 0
            there = w.at[sec, pl.ds(at, tall)]
            pltpu.make_async_copy(ref.at[pl.ds(start, tall)], there, in_sem.at[sec, i]).start()

    @pl.when(side == 0)
    def _():
        load(0, own_w)
        load(1, other_w)

    @pl.when(side != 0)
    def _():
        load(0, other_w)
        load(1, own_w)

    tall = rows if rows else width
    g_copy.start()

    starts = [sum(groups[:i]) for i in range(len(groups))]

    def turn_of(index):
        if not rows:
            return index
        away = (ring_spot(jnp.int32(index), count) - me + count) % count - count // 2
        return jnp.where(away < 0, -2 * away - 1, 2 * away)

    def emit(sec, part, value):
        for b in range(width // tall):
            here = pl.ds(pl.multiple_of(turn_of(part * (width // tall) + b) * tall, 16), tall)
            piece = value[b * tall : (b + 1) * tall]
            own_g[sec, here] = piece
            other_g[sec, here] = piece.astype(BF16)

    def send(sec, parts):
        for index in [part * (width // tall) + b for part in parts for b in range(width // tall)]:
            turn = turn_of(index)
            here = pl.ds(pl.multiple_of(turn * tall, 16), tall)

            @pl.when(side == sec)
            def _():
                pltpu.make_async_copy(own_g.at[sec, here], own_out.at[here], out_sem.at[0, index]).start()

            for start, blocks, out in zip(starts, groups, other_outs):

                @pl.when((side != sec) & (turn >= start) & (turn < start + blocks))
                def _():
                    there = pl.ds(pl.multiple_of((turn - start) * tall, 16), tall)
                    pltpu.make_async_copy(other_g.at[sec, here], out.at[there], out_sem.at[1, index]).start()

    def sent():
        for index in range(4 * width // tall):
            here = pl.ds(0, tall)
            pltpu.make_async_copy(own_g.at[0, here], own_out.at[here], out_sem.at[0, index]).wait()
            pltpu.make_async_copy(other_g.at[0, here], other_outs[0], out_sem.at[1, index]).wait()

    dims = (micro, length, width)

    def arrived(sec):
        for i, (ref, (slot, shift, start, tall)) in enumerate(own_w):
            there = w.at[sec, pl.ds(0, tall)]
            pltpu.make_async_copy(ref.at[pl.ds(start, tall)], there, in_sem.at[sec, i]).wait()

    live_copy.wait()
    x_copy.wait()
    arrived(0)
    forward(0, *dims, live_ref, x_ref, w, q_t, k, v, tr, p, mixed_t, xhat, rstd, hid)
    arrived(1)
    forward(1, *dims, live_ref, hid, w, q_t, k, v, tr, p, mixed_t, xhat, rstd, None)
    g_copy.wait()
    pieces = []
    for seq in range(micro):
        pos = lax.broadcasted_iota(jnp.int32, (length, width), 0)
        piece = g_ref[seq * length : (seq + 1) * length].astype(F32)
        pieces.append(jnp.where(pos < live_ref[0, seq], piece, 0.0))
    grad = jnp.concatenate(pieces, axis=0)
    back = backward(1, *dims, grad, hid, w, q_t, k, v, tr, p, mixed_t, xhat, rstd, g_t, dq_t, dk, dv, emit, None)
    send(1, (0, 1, 2, 3))
    backward(0, *dims, back.astype(F32), x_ref, w, q_t, k, v, tr, p, mixed_t, xhat, rstd, g_t, dq_t, dk, dv, emit, send)
    send(0, (2,))
    sent()


def run_layers(live, x, target, own, other, plan, groups, rows, count, micro, length, width):
    tokens = micro * length
    heads = width // HEAD
    hbm = pl.BlockSpec(memory_space=pl.ANY)
    far = pl.BlockSpec(memory_space=pltpu.HBM)
    first = rows if rows else width
    return pl.pallas_call(
        functools.partial(layers, micro, length, width, rows, count, plan, groups),
        out_shape=(
            jax.ShapeDtypeStruct((4 * width, width), F32),
            *[jax.ShapeDtypeStruct((blocks * first, width), BF16) for blocks in groups],
        ),
        in_specs=[far, far, hbm] + [hbm] * (len(own) + len(other)),
        out_specs=(hbm,) * (1 + len(groups)),
        scratch_shapes=[
            pltpu.SMEM((1, micro), jnp.int32),
            pltpu.VMEM((tokens, width), BF16),
            pltpu.VMEM((tokens, width), BF16),
            pltpu.VMEM((2, 4 * width, width), BF16),
            pltpu.VMEM((2, 4 * width, width), F32),
            pltpu.VMEM((2, 4 * width, width), BF16),
            pltpu.VMEM((tokens, width), BF16),
            pltpu.VMEM((2, width, tokens), BF16),
            pltpu.VMEM((2, tokens, width), BF16),
            pltpu.VMEM((2, tokens, width), BF16),
            pltpu.VMEM((width, tokens), BF16),
            pltpu.VMEM((2, micro * heads, length, length), F32),
            pltpu.VMEM((2, width, tokens), F32),
            pltpu.VMEM((2, tokens, width), F32),
            pltpu.VMEM((2, tokens, PAIR), F32),
            pltpu.VMEM((width, tokens), BF16),
            pltpu.VMEM((width, tokens), BF16),
            pltpu.VMEM((tokens, width), BF16),
            pltpu.VMEM((tokens, width), BF16),
            pltpu.SemaphoreType.DMA((2, sum(len(part) for part in plan[0]))),
            pltpu.SemaphoreType.DMA((2, 4 * width // first)),
            pltpu.SemaphoreType.DMA((3,)),
        ],
        compiler_params=pltpu.CompilerParams(vmem_limit_bytes=40 * 1024 * 1024),
    )(pltpu.with_memory_space_constraint(live, pltpu.HBM), pltpu.with_memory_space_constraint(x, pltpu.HBM), target, *own, *other)


def swapped(value):
    return lax.ppermute(value, "pipe", [(0, 1), (1, 0)])


def ring_order(count):
    return list(range(0, count, 2)) + list(range(count - 1, 0, -2))


def on_device(inputs, out_grad, lengths, master, moment_first, moment_second):
    count = lax.axis_size("dp")
    weights = master[0]
    rows, width = weights.shape
    micro, length = inputs.shape[1:3]
    ringed = count == 8 and rows % 32 == 0 and width % rows == 0
    ring = ring_order(count)
    onward = [(ring[i], ring[(i + 1) % count]) for i in range(count)]
    backward_way = [(b, a) for a, b in onward]

    def ahead(value):
        return lax.ppermute(value, "dp", onward)

    def behind(value):
        return lax.ppermute(value, "dp", backward_way)

    mine = weights.astype(BF16)
    target = out_grad[0].reshape(micro * length, width)
    x = inputs[0].reshape(micro * length, width)
    half = rows // 2
    mid = count // 2
    if ringed:
        own, plan_own = [mine], [((0, 0, 0, rows),)]
        fore, aft = mine, mine
        target, other, plan_other = swapped(target), [swapped(mine)], [((0, 0, 0, rows),)]
        for step in range(1, mid + 1):
            last = step == mid
            size = half if last else rows
            fore, aft = ahead(fore[:half] if last else fore), behind(aft[half:] if last else aft)
            own += [fore, aft]
            places = ((count - step, 0), (step, half if last else 0))
            plan_own += [((*place, 0, size),) for place in places]
            if last:
                other += [swapped(fore), swapped(aft)]
                plan_other += [((*place, 0, size),) for place in places]
            else:
                other.append(swapped(jnp.concatenate([fore, aft], axis=0)))
                plan_other.append(tuple((*place, i * size, size) for i, place in enumerate(places)))
    else:
        own = [lax.all_gather(mine, "dp", axis=0, tiled=True)]
        target, other = swapped(target), [swapped(own[0])]
        plan_own = plan_other = [((0, 0, 0, 4 * width),)]
    plan = (tuple(plan_own), tuple(plan_other))
    groups = (1, count - 1) if ringed else (4,)
    own_g, *far_g = run_layers(
        lengths, x, target, own, other, plan, groups, rows if ringed else 0, count, micro, length, width
    )
    far_g[0] = swapped(far_g[0])
    if ringed:
        near = (own_g[:rows] + far_g[0].astype(F32)).astype(BF16)
        far_g[1], near = lax.optimization_barrier((far_g[1], near))
        fore, aft = ahead(near[:half]), behind(near[half:])
        far = swapped(far_g[1])

        def block(index):
            at = index * rows
            return own_g[at : at + rows] + far[at - rows : at].astype(F32)

        for step in range(1, mid):
            up, down = block(2 * step - 1), block(2 * step)
            if step == 1:
                up = jnp.concatenate([up[:half] + fore.astype(F32), up[half:]], axis=0)
                down = jnp.concatenate([down[:half], down[half:] + aft.astype(F32)], axis=0)
            else:
                up, down = up + fore.astype(F32), down + aft.astype(F32)
            fore, aft = lax.optimization_barrier((up.astype(BF16), down.astype(BF16)))
            fore, aft = ahead(fore), behind(aft)
        terms = ((own_g, (count - 1) * rows), (far, (count - 2) * rows), (fore, 0), (aft, 0))
    else:
        total = own_g + far_g[0].astype(F32)
        terms = ((lax.psum_scatter(total, "dp", scatter_dimension=0, tiled=True), 0),)
    new_first, new_second, update, squares = run_moments(weights, moment_first[0], moment_second[0], terms)
    if ringed:
        hop = 1
        while 2 * hop < count:
            squares = squares + lax.ppermute(squares, "dp", [(i, i ^ hop) for i in range(count)])
            hop *= 2
        pair = (squares, lax.ppermute(squares, "dp", [(i, i ^ hop) for i in range(count)]))
    else:
        pair = (lax.psum(squares, "dp"),)
    new_master = run_master(weights, update, pair)
    return (new_master[None], new_first[None], new_second[None])


def moments(starts, w_in, first_in, second_in, *refs):
    count = len(starts)
    terms_in, refs = refs[:count], refs[count:]
    outs_out, squares_out, refs = refs[:3], refs[3], refs[4:]
    weights, first, second = refs[:3]
    terms, outs, squares, in_sem, out_sem = refs[3 : 3 + count], refs[3 + count : 6 + count], *refs[6 + count :]
    rows, width = weights.shape
    loads = [
        pltpu.make_async_copy(src, dst, in_sem.at[i])
        for i, (src, dst) in enumerate(
            [(src.at[pl.ds(at, rows)], dst) for src, at, dst in zip(terms_in, starts, terms)]
            + [(w_in, weights), (first_in, first), (second_in, second)]
        )
    ]
    for copy in loads:
        copy.start()
    for copy in loads:
        copy.wait()
    pieces = CUTS if rows % (CUTS * 8) == 0 else 1
    tall = rows // pieces
    sums = [jnp.zeros((8, 128), F32), jnp.zeros((8, 128), F32)]
    stores = []
    for piece in range(pieces):
        here = slice(piece * tall, (piece + 1) * tall)
        grad = terms[0][here]
        for term in terms[1:]:
            grad = grad + term[here].astype(F32)
        new_first = 0.9 * first[here] + 0.1 * grad
        new_second = 0.999 * second[here] + 0.001 * grad * grad
        corrected = new_first * (1.0 / (1.0 - 0.9**STEP))
        spread = new_second * (1.0 / (1.0 - 0.999**STEP))
        update = corrected / (jnp.sqrt(spread) + 1e-06) + 0.05 * weights[here]
        for index, value in enumerate((new_first, new_second, update)):
            outs[index][here] = value
            copy = pltpu.make_async_copy(outs[index].at[here], outs_out[index].at[here], out_sem.at[index, piece])
            copy.start()
            stores.append(copy)
        for index, value in enumerate((weights[here], update)):
            square = jnp.sum((value * value).reshape(tall // 8, 8, width), axis=0)
            for start in range(0, width, 128):
                sums[index] = sums[index] + square[:, start : start + 128]
    squares[...] = jnp.concatenate(sums, axis=0)
    copy = pltpu.make_async_copy(squares, squares_out, in_sem.at[0])
    copy.start()
    for store in stores + [copy]:
        store.wait()


def run_moments(weights, first, second, terms):
    free = pl.BlockSpec(memory_space=pl.ANY)
    rows, width = weights.shape
    same = jax.ShapeDtypeStruct(weights.shape, F32)
    return pl.pallas_call(
        functools.partial(moments, tuple(at for _, at in terms)),
        out_shape=(same, same, same, jax.ShapeDtypeStruct((16, 128), F32)),
        in_specs=[free] * (3 + len(terms)),
        out_specs=(free,) * 4,
        scratch_shapes=[pltpu.VMEM((rows, width), F32)] * 3
        + [pltpu.VMEM((rows, width), term.dtype) for term, _ in terms]
        + [pltpu.VMEM((rows, width), F32)] * 3
        + [
            pltpu.VMEM((16, 128), F32),
            pltpu.SemaphoreType.DMA((3 + len(terms),)),
            pltpu.SemaphoreType.DMA((3, CUTS)),
        ],
        compiler_params=pltpu.CompilerParams(vmem_limit_bytes=12 * 1024 * 1024),
    )(weights, first, second, *[term for term, _ in terms])


def master_step(w_in, update_in, *refs):
    count = (len(refs) - 5) // 2
    squares_in, out, refs = refs[:count], refs[count], refs[count + 1 :]
    weights, update, squares, in_sem, out_sem = refs[0], refs[1], refs[2 : 2 + count], *refs[2 + count :]
    loads = [
        pltpu.make_async_copy(src, dst, in_sem.at[i])
        for i, (src, dst) in enumerate([*zip(squares_in, squares), (w_in, weights), (update_in, update)])
    ]
    for copy in loads:
        copy.start()
    for copy in loads:
        copy.wait()
    total = squares[0][...]
    for more in squares[1:]:
        total = total + more[...]
    weight_sq = jnp.sum(total[:8], axis=(0, 1), keepdims=True)
    update_sq = jnp.sum(total[8:], axis=(0, 1), keepdims=True)
    trust = jnp.sqrt(weight_sq) / (jnp.sqrt(update_sq) + 1e-06)
    rows, width = weights.shape
    pieces = CUTS if rows % (CUTS * 8) == 0 else 1
    stores = []
    for piece in range(pieces):
        here = slice(piece * rows // pieces, (piece + 1) * rows // pieces)
        update[here] = weights[here] - 0.05 * trust * update[here]
        copy = pltpu.make_async_copy(update.at[here], out.at[here], out_sem.at[piece])
        copy.start()
        stores.append(copy)
    for copy in stores:
        copy.wait()


def run_master(weights, update, pair):
    free = pl.BlockSpec(memory_space=pl.ANY)
    rows, width = weights.shape
    return pl.pallas_call(
        master_step,
        out_shape=jax.ShapeDtypeStruct(weights.shape, F32),
        in_specs=[free] * (2 + len(pair)),
        out_specs=free,
        scratch_shapes=[pltpu.VMEM((rows, width), F32)] * 2
        + [pltpu.VMEM((16, 128), F32)] * len(pair)
        + [pltpu.SemaphoreType.DMA((2 + len(pair),)), pltpu.SemaphoreType.DMA((CUTS,))],
        compiler_params=pltpu.CompilerParams(vmem_limit_bytes=6 * 1024 * 1024),
    )(weights, update, *pair)


def solution(mesh):
    rows = P("pipe", ("groups", "dp"), None)
    in_specs = (
        P("pipe", ("groups", "dp"), None, None),
        P("pipe", ("groups", "dp"), None, None),
        P("pipe", ("groups", "dp")),
        rows,
        rows,
        rows,
    )
    return jax.shard_map(
        on_device, mesh=mesh, in_specs=in_specs, out_specs=(rows, rows, rows), check_vma=False
    )
```
